32 devices in a mesh: group: 2 (over x), space: 16 (over z, y, core).
Axes of the slice: x: 2, y: 2, z: 4, core: 2. Of those that a mesh axis runs over, the one named last changes fastest.
Arguments:
- states: float32 [4, 69, 384, 128], P('group', None, 'space'), parts along dimension 0, may hold values from -6 to 6
- plan: int32 [4], P('group'), parts along dimension 0, may hold values from 0 to 1, each once
- member_ids: int32 [4], P('group'), parts along dimension 0, may hold values from 0 to 15
- member_table: float32 [16, 512], replicated, may hold values from -6 to 6
- enc_weight: bfloat16 [3, 3, 69, 512], replicated, may hold values from -0.25 to 0.25
- proc_weight: bfloat16 [2, 3, 3, 512, 512], replicated, may hold values from -0.09375 to 0.09375
- dec_weight: bfloat16 [3, 3, 512, 69], replicated, may hold values from -0.1875 to 0.1875
Outputs:
- forecasts: float32 [2, 4, 69, 384, 128], P(None, 'group', None, 'space'), parts along dimension 1
The draws below stay inside these ranges and needn't reach their ends.
There are 2 independent parts, one for each index of `group`. The reference program is written for one: setup_inputs(seed, part) draws one part's arguments, and reference() takes and returns one part's arrays. A program takes and returns all parts, laid end to end along the dimension named above; an argument that names none is the same for every part. Nothing has to cross between parts.
Inputs may be any that keep to these rules, and one draw needn't show every extreme that they name: plan is a permutation of the 2 member slots. member_ids index rows of member_table.
All inputs are finite; a program needn't handle non-finite values.
Results may differ from the reference program's by a relative error of at most 0.012.
Values may be sent and summed in bfloat16 or wider, within the bound.
No kernel may reach another device: no remote copies, remote signals or barrier semaphores. Data moves between devices by JAX's collectives and lax.ppermute only.
A program may use at most 128 MiB of HBM per device.

```python
import jax
import jax.numpy as jnp

VARS = 69
HID = 512
LAT = 128
MEMB = 2
ENS = 16
LAYERS = 2
STEPS = 2
LON = 384


def levels(rng, dims, shards, least, high):
    def one(dim, parts):
        heights = jax.random.uniform(jax.random.fold_in(jax.random.fold_in(rng, 6), dim), (parts,), jnp.float32, least / len(shards), high / len(shards))
        return jnp.repeat(jnp.exp(heights), dims[dim] // parts).reshape((-1,) + (1,) * (len(dims) - dim - 1))

    level = one(*shards[0])
    for cut in shards[1:]:
        level = level * one(*cut)
    return level


def centred(key, shape, scale, bound, cuts=(), dtype=jnp.bfloat16):
    result = scale * jax.random.normal(key, shape, jnp.float32)
    if cuts:
        result = result * levels(key, shape, cuts, -0.22, 0.18)
    return jnp.clip(result, -bound, bound).astype(dtype)


def setup_inputs(seed: int = 0, part: int = 0) -> dict:
    arg_keys = jax.random.split(jax.random.key(seed), 8)
    part_keys = jax.random.split(jax.random.fold_in(arg_keys[7], part), 8)
    states = centred(part_keys[0], (MEMB, VARS, LON, LAT), 1.0, 6.0, ((2, 16),), jnp.float32)
    plan = jax.random.permutation(part_keys[1], MEMB).astype(jnp.int32)
    member_ids = jax.random.randint(part_keys[2], (MEMB,), 0, ENS).astype(jnp.int32)
    member_table = centred(arg_keys[3], (ENS, HID), 1.0, 6.0, (), jnp.float32)
    enc_weight = centred(arg_keys[4], (3, 3, VARS, HID), (9 * VARS) ** -0.5, 0.25)
    proc_weight = centred(arg_keys[5], (LAYERS, 3, 3, HID, HID), (9 * HID) ** -0.5, 0.09375)
    dec_weight = centred(arg_keys[6], (3, 3, HID, VARS), (2 * HID) ** -0.5, 0.1875)
    return {"states": states, "plan": plan, "member_ids": member_ids, "member_table": member_table, "enc_weight": enc_weight, "proc_weight": proc_weight, "dec_weight": dec_weight}


parity_taps = (((1, 0),), ((2, 0), (0, 1)))


def activate(values):
    return jax.nn.gelu(values.astype(jnp.float32), approximate=True).astype(jnp.bfloat16)


def encode(field, member_vecs, enc_weight):
    lon_cells = field.shape[2] // 2
    lat_cells = field.shape[3] // 2
    rounded = field.astype(jnp.bfloat16)
    padded = jnp.concatenate([rounded[:, :, -1:], rounded], axis=2)
    padded = jnp.pad(padded, ((0, 0), (0, 0), (0, 0), (1, 0)))
    summed = jnp.broadcast_to(member_vecs[:, None, None, :].astype(jnp.float32),
                              (field.shape[0], lon_cells, lat_cells, member_vecs.shape[1]))
    for a in range(3):
        for b in range(3):
            window = padded[:, :, a:a + 2 * lon_cells:2, b:b + 2 * lat_cells:2]
            summed = summed + jnp.einsum("mvxy,vh->mxyh", window.astype(jnp.float32),
                                         enc_weight[a, b].astype(jnp.float32))
    return summed.astype(jnp.bfloat16)


def process(hidden, proc_weight):
    lon_cells = hidden.shape[1]
    lat_cells = hidden.shape[2]
    for layer_index in range(LAYERS):
        dilation = layer_index + 1
        active = activate(hidden)
        padded = jnp.concatenate([active[:, -dilation:], active, active[:, :dilation]], axis=1)
        padded = jnp.pad(padded, ((0, 0), (0, 0), (dilation, dilation), (0, 0)))
        summed = hidden.astype(jnp.float32)
        for a in range(3):
            for b in range(3):
                window = padded[:, a * dilation:a * dilation + lon_cells, b * dilation:b * dilation + lat_cells]
                summed = summed + jnp.einsum("mxyh,hk->mxyk", window.astype(jnp.float32),
                                             proc_weight[layer_index, a, b].astype(jnp.float32))
        hidden = summed.astype(jnp.bfloat16)
    return hidden


def decode(hidden, dec_weight):
    lon_cells = hidden.shape[1]
    lat_cells = hidden.shape[2]
    outgoing = activate(hidden)
    padded = jnp.concatenate([outgoing, outgoing[:, :1]], axis=1)
    padded = jnp.pad(padded, ((0, 0), (0, 0), (0, 1), (0, 0)))
    products = {}
    for a in range(3):
        for b in range(3):
            products[(a, b)] = jnp.einsum("mxyh,hv->mvxy", padded.astype(jnp.float32),
                                          dec_weight[a, b].astype(jnp.float32))
    columns = []
    for lon_parity in range(2):
        rows = []
        for lat_parity in range(2):
            summed = jnp.zeros(products[(0, 0)].shape[:2] + (lon_cells, lat_cells), jnp.float32)
            for lon_tap, lon_step in parity_taps[lon_parity]:
                for lat_tap, lat_step in parity_taps[lat_parity]:
                    summed = summed + products[(lon_tap, lat_tap)][:, :, lon_step:lon_step + lon_cells,
                                                                   lat_step:lat_step + lat_cells]
            rows.append(summed)
        stacked = jnp.stack(rows, axis=-1)
        columns.append(stacked.reshape(stacked.shape[0], stacked.shape[1], lon_cells, 2 * lat_cells))
    stacked = jnp.stack(columns, axis=3)
    return stacked.reshape(stacked.shape[0], stacked.shape[1], 2 * lon_cells, 2 * lat_cells)


def reference(states, plan, member_ids, member_table, enc_weight, proc_weight, dec_weight):
    field = states[plan]
    slot_ids = member_ids[plan]
    member_vecs = member_table[slot_ids]
    results = []
    for step_index in range(STEPS):
        hidden = encode(field, member_vecs, enc_weight)
        hidden = process(hidden, proc_weight)
        field = field + decode(hidden, dec_weight)
        results.append(field)
    return jnp.stack(results)
```

```python
import functools

import jax
import jax.numpy as jnp
from jax import lax
from jax.experimental import pallas as pl
from jax.experimental.pallas import tpu as pltpu
from jax.sharding import PartitionSpec as P

STEPS = 2
VPAD = 80
WEST = 7
EAST = 8
F32 = jnp.float32
BF16 = jnp.bfloat16


def chunks(total, size):
    count = max(1, total // size)
    base, extra = divmod(total, count)
    start, out = 0, []
    for k in range(count):
        n = base + (1 if k < extra else 0)
        out.append((start, n))
        start += n
    return out


def gelu(x):
    inner = x * (0.7978845608028654 + 0.035677408136300125 * (x * x))
    half = 0.5 * x
    return half + half * jnp.tanh(inner)


def nt_dot(lhs, rhs):
    return lax.dot_general(lhs, rhs, (((1,), (1,)), ((), ())), preferred_element_type=F32)


def dot(lhs, rhs):
    return jnp.dot(lhs, rhs, preferred_element_type=F32)


def step_kernel(first, step, member, dims, *refs):
    nvars, cols, lat, hid = dims
    half = lat // 2
    coarse = cols // 2
    refs = list(refs)
    plan_ref, ids_ref = refs[:2]
    field_hbm, own_hbm, west_hbm, east_hbm = refs[2:6]
    table_ref, wenc_ref, wproc_hbm, wdec_ref = refs[6:10]
    refs = refs[10:]
    if not (first and member == 0):
        refs = refs[1:]
    out_hbm = refs[0]
    refs = refs[1:]
    if first:
        own_ref, wedge_ref, eedge_ref = refs[:3]
        refs = refs[3:]
    (fld, west, east, own, wproc, tmp, xe, xo, x1, x2, h0, h1, oo, d_ref, act, sems) = refs

    slot = plan_ref[member]
    if first:
        load_field = pltpu.make_async_copy(field_hbm.at[slot], fld, sems.at[0])
        load_west = pltpu.make_async_copy(west_hbm.at[slot], west, sems.at[1])
        load_east = pltpu.make_async_copy(east_hbm.at[slot], east, sems.at[2])
    else:
        load_field = pltpu.make_async_copy(out_hbm.at[step - 1, member], fld, sems.at[0])
        load_west = pltpu.make_async_copy(west_hbm, west, sems.at[1])
        load_east = pltpu.make_async_copy(east_hbm, east, sems.at[2])
        load_own = pltpu.make_async_copy(own_hbm, own, sems.at[3])
        load_own.start()
    load_field.start()
    load_west.start()
    load_east.start()
    load_w = [
        pltpu.make_async_copy(wproc_hbm.at[layer], wproc.at[layer], sems.at[4 + layer])
        for layer in range(2)
    ]
    load_w[0].start()
    load_w[1].start()

    always = plan_ref[0] >= 0
    mvec = table_ref[pl.ds(ids_ref[slot], 1), :]
    pick = (
        lax.broadcasted_iota(jnp.int32, (half, lat), 1)
        == 2 * lax.broadcasted_iota(jnp.int32, (half, lat), 0) + 1
    ).astype(F32).astype(BF16)
    lane = lax.broadcasted_iota(jnp.int32, (VPAD, lat), 1)
    tmp[...] = jnp.zeros(tmp.shape, F32)

    def take_in(index, values):
        one = pltpu.roll(values, 1, 1)
        two = jnp.where(lane < 2, 0.0, pltpu.roll(values, 2, 1))
        stacked = jnp.concatenate(
            [values, one, two, jnp.zeros((256 - 3 * VPAD, lat), F32)], axis=0
        ).astype(BF16)
        picked = nt_dot(pick, stacked).astype(BF16)
        target = xe if index % 2 == 0 else xo
        target[(index // 2) * half : (index // 2 + 1) * half, :] = picked

    if first:
        load_field.wait()
    else:
        load_own.wait()
    for p in range(cols):
        if first:
            buf = p % 4
            tmp[buf, 0:nvars, :] = fld[pl.ds(p, nvars, stride=cols), :]
            values = tmp[buf]
        else:
            values = own[p].astype(F32)
        take_in(WEST + p, values)
    load_west.wait()
    for p in range(WEST):
        take_in(p, west[p].astype(F32))
    load_east.wait()
    for p in range(EAST):
        take_in(WEST + cols + p, east[p].astype(F32))

    def spread(values, ncols, start, dilation, target):
        rows = lax.broadcasted_iota(jnp.int32, (ncols * half, hid), 0) & (half - 1)
        down = jnp.where(rows < dilation, 0.0, pltpu.roll(values, dilation, 0))
        up = jnp.where(
            rows >= half - dilation, 0.0, pltpu.roll(values, ncols * half - dilation, 0)
        )
        where = slice(start * half, (start + ncols) * half)
        target[where, 0:hid] = down.astype(BF16)
        target[where, hid : 2 * hid] = values.astype(BF16)
        target[where, 2 * hid : 3 * hid] = up.astype(BF16)


    @pl.when(always)
    def encode():
        for start, n in chunks(coarse + 7, 4):
            rows = slice(start * half, (start + n) * half)
            after = slice((start + 1) * half, (start + 1 + n) * half)
            hidden = dot(xe[rows, :], wenc_ref[0]) + dot(xo[rows, :], wenc_ref[1])
            hidden = hidden + dot(xe[after, :], wenc_ref[2]) + mvec
            lo, hi = max(start, 1), min(start + n, coarse + 6)
            h0[(lo - 1) * half : (hi - 1) * half, :] = hidden[
                (lo - start) * half : (hi - start) * half
            ]
            spread(gelu(hidden), n, start, 1, x1)

    load_w[0].wait()

    @pl.when(always)
    def layer0():
        for start, n in chunks(coarse + 5, 4):
            hidden = h0[start * half : (start + n) * half, :]
            for a in range(3):
                hidden = hidden + dot(x1[(start + a) * half : (start + a + n) * half, :], wproc[0, a])
            lo, hi = max(start, 2), min(start + n, coarse + 3)
            h1[(lo - 2) * half : (hi - 2) * half, :] = hidden[
                (lo - start) * half : (hi - start) * half
            ]
            spread(gelu(hidden), n, start, 2, x2)

    load_w[1].wait()

    @pl.when(always)
    def layer1():
        for start, n in chunks(coarse + 1, 4):
            hidden = h1[start * half : (start + n) * half, :]
            for a in range(3):
                hidden = hidden + dot(
                    x2[(start + 2 * a) * half : (start + 2 * a + n) * half, :], wproc[1, a]
                )
            outgoing = gelu(hidden)
            rows = lax.broadcasted_iota(jnp.int32, (n * half, hid), 0) & (half - 1)
            up = jnp.where(rows >= half - 1, 0.0, pltpu.roll(outgoing, n * half - 1, 0))
            where = slice(start * half, (start + n) * half)
            oo[where, 0:hid] = outgoing.astype(BF16)
            oo[where, hid : 2 * hid] = up.astype(BF16)

    if not first:
        load_field.wait()

    @pl.when(always)
    def decode():
        key = lax.broadcasted_iota(jnp.int32, (2 * lat, 2 * lat), 0)
        spot = (key // half % 2) * lat + 2 * (key % half) + key // lat
        weave = (lax.broadcasted_iota(jnp.int32, (2 * lat, 2 * lat), 1) == spot).astype(F32).astype(BF16)
        v = VPAD
        for start, n in chunks(coarse // 2, 2):
            start, n = 2 * start, 2 * n
            here = slice(start * half, (start + n) * half)
            nxt = slice((start + 1) * half, (start + 1 + n) * half)
            g1 = nt_dot(wdec_ref[0 : 4 * v], oo[here, 0:hid])
            g2 = nt_dot(wdec_ref[4 * v : 6 * v], oo[here, hid : 2 * hid])
            g3 = nt_dot(wdec_ref[6 * v : 8 * v], oo[nxt, 0:hid])
            g4 = nt_dot(wdec_ref[8 * v : 9 * v], oo[nxt, hid : 2 * hid])
            parts = (
                (g1[0:v], g1[v : 2 * v] + g2[0:v]),
                (
                    g1[2 * v : 3 * v] + g3[0:v],
                    g1[3 * v : 4 * v] + g2[v : 2 * v] + g3[v : 2 * v] + g4,
                ),
            )
            for pair in range(n // 2):
                lanes = slice(pair * lat, (pair + 1) * lat)
                for lon_parity in range(2):
                    even, odd = parts[lon_parity]
                    both = jnp.concatenate([even[:, lanes], odd[:, lanes]], axis=1).astype(BF16)
                    woven = dot(both, weave)
                    for side in range(2):
                        p = 2 * (start + 2 * pair + side) + lon_parity
                        update = woven[:, side * lat : (side + 1) * lat]
                        there = pl.ds(p, nvars, stride=cols)
                        value = fld[there, :] + update[0:nvars]
                        fld[there, :] = value
                        if first:
                            buf = p % 4
                            tmp[buf, 0:nvars, :] = value
                            rounded = tmp[buf].astype(BF16)
                            own_ref[p] = rounded
                            if p < EAST:
                                wedge_ref[p] = rounded
                            if p >= cols - WEST:
                                eedge_ref[p - (cols - WEST)] = rounded

    save = pltpu.make_async_copy(fld, out_hbm.at[step, member], sems.at[6])
    save.start()
    save.wait()


def run_step(step, member, dims, members, plan, ids, field, own, west, east, table, wenc, wproc, wdec, buf):
    nvars, cols, lat, hid = dims
    half, coarse = lat // 2, cols // 2
    first = step == 0
    smem = pl.BlockSpec(memory_space=pltpu.SMEM)
    hbm = pl.BlockSpec(memory_space=pl.ANY)
    vmem = pl.BlockSpec(memory_space=pltpu.VMEM)
    args = [plan, ids, field, own, west, east, table, wenc, wproc, wdec]
    in_specs = [smem, smem, hbm, hbm, hbm, hbm, vmem, vmem, hbm, vmem]
    aliases = {}
    if buf is not None:
        aliases = {len(args): 0}
        args.append(buf)
        in_specs.append(hbm)
    out_shape = [jax.ShapeDtypeStruct((STEPS, members, nvars * cols, lat), F32)]
    out_specs = [hbm]
    if first:
        for n in (cols, EAST, WEST):
            out_shape.append(jax.ShapeDtypeStruct((n, VPAD, lat), BF16))
            out_specs.append(vmem)
    scratch = [
        pltpu.VMEM((nvars * cols, lat), F32),
        pltpu.VMEM((WEST, VPAD, lat), BF16),
        pltpu.VMEM((EAST, VPAD, lat), BF16),
        pltpu.VMEM((cols if not first else 1, VPAD, lat), BF16),
        pltpu.VMEM(wproc.shape, BF16),
        pltpu.VMEM((4, VPAD, lat), F32),
        pltpu.VMEM(((coarse + 8) * half, 256), BF16),
        pltpu.VMEM(((coarse + 7) * half, 256), BF16),
        pltpu.VMEM(((coarse + 7) * half, 3 * hid), BF16),
        pltpu.VMEM(((coarse + 5) * half, 3 * hid), BF16),
        pltpu.VMEM(((coarse + 5) * half, hid), F32),
        pltpu.VMEM(((coarse + 1) * half, hid), F32),
        pltpu.VMEM(((coarse + 1) * half, 2 * hid), BF16),
        pltpu.VMEM((8, lat), F32),
        pltpu.VMEM((8, lat), F32),
        pltpu.SemaphoreType.DMA((8,)),
    ]
    flops = 2 * half * hid * hid * 9 * (2 * coarse + 6)
    return pl.pallas_call(
        functools.partial(step_kernel, first, step, member, dims),
        out_shape=out_shape,
        in_specs=in_specs,
        out_specs=out_specs,
        scratch_shapes=scratch,
        input_output_aliases=aliases,
        cost_estimate=pl.CostEstimate(flops=flops, bytes_accessed=12 * 2**20, transcendentals=0),
        compiler_params=pltpu.CompilerParams(vmem_limit_bytes=56 * 2**20),
        name="step%d_member%d" % (step, member),
    )(*args)


def exchange(last, first):
    count = lax.axis_size("space")
    forward = [(i, (i + 1) % count) for i in range(count)]
    backward = [(target, source) for source, target in forward]
    return lax.ppermute(last, "space", forward), lax.ppermute(first, "space", backward)


def local(states, plan, member_ids, member_table, enc_weight, proc_weight, dec_weight):
    members, nvars, cols, lat = states.shape
    hid = proc_weight.shape[-1]
    dims = (nvars, cols, lat, hid)

    pad_v = ((0, 0), (0, 0), (0, VPAD - nvars), (0, 0))
    wenc = jnp.pad(enc_weight[:, ::-1], pad_v).reshape(3, 3 * VPAD, hid)
    wenc = jnp.pad(wenc, ((0, 0), (0, 256 - 3 * VPAD), (0, 0)))
    taps = ((1, 1), (1, 2), (2, 1), (2, 2), (1, 0), (2, 0), (0, 1), (0, 2), (0, 0))
    wdec = jnp.stack([dec_weight[a, b] for a, b in taps])
    wdec = jnp.pad(jnp.transpose(wdec, (0, 2, 1)), ((0, 0), (0, VPAD - nvars), (0, 0)))
    wdec = wdec.reshape(9 * VPAD, hid)
    wproc = proc_weight.reshape(proc_weight.shape[0], 3, 3 * hid, hid)

    def edge(part):
        part = jnp.transpose(part, (0, 2, 1, 3)).astype(BF16)
        return jnp.pad(part, pad_v)

    west, east = exchange(edge(states[:, :, cols - WEST :]), edge(states[:, :, :EAST]))
    flat = states.reshape(members, nvars * cols, lat)
    run = functools.partial(run_step, dims=dims, members=members, plan=plan, ids=member_ids,
                            table=member_table, wenc=wenc, wproc=wproc, wdec=wdec)
    buf = None
    halos = []
    for m in range(members):
        buf, own, first, last = run(0, m, field=flat, own=west, west=west, east=east, buf=buf)
        halos.append((own,) + exchange(last, first))
    for m in range(members):
        own, west, east = halos[m]
        (buf,) = run(1, m, field=flat, own=own, west=west, east=east, buf=buf)
    return buf.reshape(STEPS, members, nvars, cols, lat)


def solution(mesh):
    return jax.shard_map(
        local,
        mesh=mesh,
        in_specs=(P("group", None, "space", None), P("group"), P("group"), P(), P(), P(), P()),
        out_specs=P(None, "group", None, "space", None),
        check_vma=False,
    )
```

```python
import functools

import jax
import jax.numpy as jnp
from jax import lax
from jax.experimental import pallas as pl
from jax.experimental.pallas import tpu as pltpu
from jax.sharding import PartitionSpec as P

STEPS = 2
VPAD = 80
WEST = 7
EAST = 8
EDGE = 8
F32 = jnp.float32
BF16 = jnp.bfloat16


def chunks(total, size):
    count = max(1, total // size)
    base, extra = divmod(total, count)
    start, out = 0, []
    for k in range(count):
        n = base + (1 if k < extra else 0)
        out.append((start, n))
        start += n
    return out


def gelu(x):
    inner = x * (0.7978845608028654 + 0.035677408136300125 * (x * x))
    half = 0.5 * x
    return half + half * jnp.tanh(inner)


def nt_dot(lhs, rhs):
    return lax.dot_general(lhs, rhs, (((1,), (1,)), ((), ())), preferred_element_type=F32)


def dot(lhs, rhs):
    return jnp.dot(lhs, rhs, preferred_element_type=F32)


def step_kernel(step, dims, *refs):
    members, nvars, cols, lat, hid = dims
    half = lat // 2
    coarse = cols // 2
    first, last = step == 0, step == STEPS - 1
    refs = list(refs)
    plan_ref, ids_ref, field_hbm, west_hbm, east_hbm = refs[:5]
    table_ref, wenc_hbm, wproc_hbm, wdec_hbm = refs[5:9]
    refs = refs[9 if first else 10 :]
    out_hbm = refs[0]
    refs = refs[1:]
    if not last:
        wedge_ref, eedge_ref = refs[:2]
        refs = refs[2:]
    (flds, west, east, wenc_ref, wproc, wdec_ref, halo) = refs[:7]
    (tmp, xe, xo, x1, x2, h0, h1, oo, sems, wsems) = refs[7:]

    def load_field(member):
        source = field_hbm.at[plan_ref[member]] if first else out_hbm.at[step - 1, member]
        return pltpu.make_async_copy(source, flds.at[member], sems.at[member])

    def save_field(member):
        return pltpu.make_async_copy(
            flds.at[member], out_hbm.at[step, member], sems.at[members + member]
        )

    load_west = pltpu.make_async_copy(west_hbm, west, wsems.at[0])
    load_east = pltpu.make_async_copy(east_hbm, east, wsems.at[1])
    load_enc = pltpu.make_async_copy(wenc_hbm, wenc_ref, wsems.at[2])
    load_dec = pltpu.make_async_copy(wdec_hbm, wdec_ref, wsems.at[3])
    load_w = [
        [
            pltpu.make_async_copy(
                wproc_hbm.at[layer, a], wproc.at[layer, a], wsems.at[4 + 3 * layer + a]
            )
            for a in range(3)
        ]
        for layer in range(2)
    ]
    load_field(0).start()
    load_west.start()
    load_east.start()
    load_enc.start()
    for load in load_w[0]:
        load.start()
    for member in range(1, members):
        load_field(member).start()

    pick = (
        lax.broadcasted_iota(jnp.int32, (half, lat), 1)
        == 2 * lax.broadcasted_iota(jnp.int32, (half, lat), 0) + 1
    ).astype(F32).astype(BF16)
    lane = lax.broadcasted_iota(jnp.int32, (VPAD, lat), 1)
    tmp[...] = jnp.zeros(tmp.shape, F32)

    def take_in(index, values):
        buf = index % tmp.shape[0]
        tmp[buf, 0:nvars, :] = values
        values = tmp[buf]
        one = pltpu.roll(values, 1, 1)
        two = jnp.where(lane < 2, 0.0, pltpu.roll(values, 2, 1))
        stacked = jnp.concatenate(
            [values, one, two, jnp.zeros((256 - 3 * VPAD, lat), F32)], axis=0
        ).astype(BF16)
        picked = nt_dot(pick, stacked).astype(BF16)
        target = xe if index % 2 == 0 else xo
        target[(index // 2) * half : (index // 2 + 1) * half, :] = picked

    def spread(values, ncols, start, dilation, target):
        rows = lax.broadcasted_iota(jnp.int32, (ncols * half, hid), 0) & (half - 1)
        down = jnp.where(rows < dilation, 0.0, pltpu.roll(values, dilation, 0))
        up = jnp.where(
            rows >= half - dilation, 0.0, pltpu.roll(values, ncols * half - dilation, 0)
        )
        where = slice(start * half, (start + ncols) * half)
        target[where, 0:hid] = down.astype(BF16)
        target[where, hid : 2 * hid] = values.astype(BF16)
        target[where, 2 * hid : 3 * hid] = up.astype(BF16)

    def roll_out(member, carry):
        slot = plan_ref[member]
        always = slot >= 0
        opening = member == 0
        fld = flds.at[member]
        mvec = table_ref[pl.ds(ids_ref[slot], 1), :]
        load_field(member).wait()

        @pl.when(opening)
        def arrive():
            load_west.wait()
            load_east.wait()

        halo[0] = west[slot if first else member].astype(F32)
        halo[1] = east[slot if first else member].astype(F32)

        @pl.when(always)
        def take_own():
            for p in range(cols):
                take_in(WEST + p, fld[pl.ds(p, nvars, stride=cols), :])
            for p in range(WEST):
                take_in(p, halo[0, pl.ds(EDGE - WEST + p, nvars, stride=EDGE), :])
            for p in range(EAST):
                take_in(WEST + cols + p, halo[1, pl.ds(p, nvars, stride=EDGE), :])

        @pl.when(opening)
        def encoder_weight():
            load_enc.wait()

        @pl.when(always)
        def encode():
            for start, n in chunks(coarse + 7, 4):
                rows = slice(start * half, (start + n) * half)
                after = slice((start + 1) * half, (start + 1 + n) * half)
                hidden = dot(xe[rows, :], wenc_ref[0]) + dot(xo[rows, :], wenc_ref[1])
                hidden = hidden + dot(xe[after, :], wenc_ref[2]) + mvec
                lo, hi = max(start, 1), min(start + n, coarse + 6)
                h0[(lo - 1) * half : (hi - 1) * half, :] = hidden[
                    (lo - start) * half : (hi - start) * half
                ]
                spread(gelu(hidden), n, start, 1, x1)

        @pl.when(opening)
        def layer0_weight():
            for load in load_w[0]:
                load.wait()
            for load in load_w[1]:
                load.start()
            load_dec.start()

        @pl.when(always)
        def layer0():
            for start, n in chunks(coarse + 5, 4):
                hidden = h0[start * half : (start + n) * half, :]
                for a in range(3):
                    hidden = hidden + dot(x1[(start + a) * half : (start + a + n) * half, :], wproc[0, a])
                lo, hi = max(start, 2), min(start + n, coarse + 3)
                h1[(lo - 2) * half : (hi - 2) * half, :] = hidden[
                    (lo - start) * half : (hi - start) * half
                ]
                spread(gelu(hidden), n, start, 2, x2)

        @pl.when(opening)
        def layer1_weight():
            for load in load_w[1]:
                load.wait()

        @pl.when(always)
        def layer1():
            for start, n in chunks(coarse + 1, 4):
                hidden = h1[start * half : (start + n) * half, :]
                for a in range(3):
                    hidden = hidden + dot(
                        x2[(start + 2 * a) * half : (start + 2 * a + n) * half, :], wproc[1, a]
                    )
                outgoing = gelu(hidden)
                rows = lax.broadcasted_iota(jnp.int32, (n * half, hid), 0) & (half - 1)
                up = jnp.where(rows >= half - 1, 0.0, pltpu.roll(outgoing, n * half - 1, 0))
                where = slice(start * half, (start + n) * half)
                oo[where, 0:hid] = outgoing.astype(BF16)
                oo[where, hid : 2 * hid] = up.astype(BF16)

        @pl.when(opening)
        def decoder_weight():
            load_dec.wait()

        @pl.when(always)
        def decode():
            key = lax.broadcasted_iota(jnp.int32, (2 * lat, 2 * lat), 0)
            spot = (key // half % 2) * lat + 2 * (key % half) + key // lat
            weave = (lax.broadcasted_iota(jnp.int32, (2 * lat, 2 * lat), 1) == spot).astype(F32).astype(BF16)
            v = VPAD
            for start, n in chunks(coarse // 2, 2):
                start, n = 2 * start, 2 * n
                here = slice(start * half, (start + n) * half)
                nxt = slice((start + 1) * half, (start + 1 + n) * half)
                g1 = nt_dot(wdec_ref[0 : 4 * v], oo[here, 0:hid])
                g2 = nt_dot(wdec_ref[4 * v : 6 * v], oo[here, hid : 2 * hid])
                g3 = nt_dot(wdec_ref[6 * v : 8 * v], oo[nxt, 0:hid])
                g4 = nt_dot(wdec_ref[8 * v : 9 * v], oo[nxt, hid : 2 * hid])
                parts = (
                    (g1[0:v], g1[v : 2 * v] + g2[0:v]),
                    (
                        g1[2 * v : 3 * v] + g3[0:v],
                        g1[3 * v : 4 * v] + g2[v : 2 * v] + g3[v : 2 * v] + g4,
                    ),
                )
                for pair in range(n // 2):
                    lanes = slice(pair * lat, (pair + 1) * lat)
                    for lon_parity in range(2):
                        even, odd = parts[lon_parity]
                        both = jnp.concatenate([even[:, lanes], odd[:, lanes]], axis=1).astype(BF16)
                        woven = dot(both, weave)
                        for side in range(2):
                            p = 2 * (start + 2 * pair + side) + lon_parity
                            update = woven[:, side * lat : (side + 1) * lat]
                            there = pl.ds(p, nvars, stride=cols)
                            value = fld[there, :] + update[0:nvars]
                            fld[there, :] = value

        save_field(member).start()
        if not last:
            for edge_ref, start in ((wedge_ref, 0), (eedge_ref, cols - EDGE)):
                rows = [fld[v * cols + start : v * cols + start + EDGE, :] for v in range(nvars)]
                edge_ref[member] = jnp.concatenate(rows, axis=0).astype(BF16)
        return carry

    lax.fori_loop(0, members, roll_out, 0)
    for member in range(members):
        save_field(member).wait()


def run_step(step, dims, plan, ids, field, west, east, table, wenc, wproc, wdec, buf):
    members, nvars, cols, lat, hid = dims
    half, coarse = lat // 2, cols // 2
    smem = pl.BlockSpec(memory_space=pltpu.SMEM)
    hbm = pl.BlockSpec(memory_space=pl.ANY)
    vmem = pl.BlockSpec(memory_space=pltpu.VMEM)
    args = [plan, ids, field, west, east, table, wenc, wproc, wdec]
    in_specs = [smem, smem, hbm, hbm, hbm, vmem, hbm, hbm, hbm]
    aliases = {}
    if buf is not None:
        aliases = {len(args): 0}
        args.append(buf)
        in_specs.append(hbm)
    out_shape = [jax.ShapeDtypeStruct((STEPS, members, nvars * cols, lat), F32)]
    out_specs = [hbm]
    if step < STEPS - 1:
        out_shape += [jax.ShapeDtypeStruct((members, nvars * EDGE, lat), BF16)] * 2
        out_specs += [vmem] * 2
    scratch = [
        pltpu.VMEM((members, nvars * cols, lat), F32),
        pltpu.VMEM((members, nvars * EDGE, lat), BF16),
        pltpu.VMEM((members, nvars * EDGE, lat), BF16),
        pltpu.VMEM(wenc.shape, BF16),
        pltpu.VMEM(wproc.shape, BF16),
        pltpu.VMEM(wdec.shape, BF16),
        pltpu.VMEM((2, nvars * EDGE, lat), F32),
        pltpu.VMEM((8, VPAD, lat), F32),
        pltpu.VMEM(((coarse + 8) * half, 256), BF16),
        pltpu.VMEM(((coarse + 7) * half, 256), BF16),
        pltpu.VMEM(((coarse + 7) * half, 3 * hid), BF16),
        pltpu.VMEM(((coarse + 5) * half, 3 * hid), BF16),
        pltpu.VMEM(((coarse + 5) * half, hid), F32),
        pltpu.VMEM(((coarse + 1) * half, hid), F32),
        pltpu.VMEM(((coarse + 1) * half, 2 * hid), BF16),
        pltpu.SemaphoreType.DMA((2 * members,)),
        pltpu.SemaphoreType.DMA((10,)),
    ]
    flops = members * 2 * half * hid * hid * 9 * (2 * coarse + 6)
    return pl.pallas_call(
        functools.partial(step_kernel, step, dims),
        out_shape=out_shape,
        in_specs=in_specs,
        out_specs=out_specs,
        scratch_shapes=scratch,
        input_output_aliases=aliases,
        cost_estimate=pl.CostEstimate(flops=flops, bytes_accessed=16 * 2**20, transcendentals=0),
        compiler_params=pltpu.CompilerParams(vmem_limit_bytes=56 * 2**20),
        name="rollout_step%d" % step,
    )(*args)


def exchange(last, first):
    count = lax.axis_size("space")
    forward = [(i, (i + 1) % count) for i in range(count)]
    backward = [(target, source) for source, target in forward]
    return lax.ppermute(last, "space", forward), lax.ppermute(first, "space", backward)


def local(states, plan, member_ids, member_table, enc_weight, proc_weight, dec_weight):
    members, nvars, cols, lat = states.shape
    hid = proc_weight.shape[-1]
    dims = (members, nvars, cols, lat, hid)

    pad_v = ((0, 0), (0, 0), (0, VPAD - nvars), (0, 0))
    wenc = jnp.pad(enc_weight[:, ::-1], pad_v).reshape(3, 3 * VPAD, hid)
    wenc = jnp.pad(wenc, ((0, 0), (0, 256 - 3 * VPAD), (0, 0)))
    taps = ((1, 1), (1, 2), (2, 1), (2, 2), (1, 0), (2, 0), (0, 1), (0, 2), (0, 0))
    wdec = jnp.stack([dec_weight[a, b] for a, b in taps])
    wdec = jnp.pad(jnp.transpose(wdec, (0, 2, 1)), ((0, 0), (0, VPAD - nvars), (0, 0)))
    wdec = wdec.reshape(9 * VPAD, hid)
    wproc = proc_weight.reshape(proc_weight.shape[0], 3, 3 * hid, hid)

    flat_edge = (members, nvars * EDGE, lat)
    west, east = exchange(
        states[:, :, cols - EDGE :].astype(BF16).reshape(flat_edge),
        states[:, :, :EDGE].astype(BF16).reshape(flat_edge),
    )
    flat = states.reshape(members, nvars * cols, lat)
    buf = None
    for step in range(STEPS):
        result = run_step(
            step, dims, plan, member_ids, flat, west, east, member_table, wenc, wproc, wdec, buf
        )
        buf = result[0]
        if step < STEPS - 1:
            west, east = exchange(result[2], result[1])
    return buf.reshape(STEPS, members, nvars, cols, lat)


def solution(mesh):
    return jax.shard_map(
        local,
        mesh=mesh,
        in_specs=(P("group", None, "space", None), P("group"), P("group"), P(), P(), P(), P()),
        out_specs=P(None, "group", None, "space", None),
        check_vma=False,
    )
```

```python
import functools

import jax
import jax.numpy as jnp
from jax import lax
from jax.experimental import pallas as pl
from jax.experimental.pallas import tpu as pltpu
from jax.sharding import PartitionSpec as P

STEPS = 2
VPAD = 80
WEST = 7
EAST = 8
EDGE = 8
KENC = 256
F32 = jnp.float32
BF16 = jnp.bfloat16


def chunks(total, size):
    count = max(1, total // size)
    base, extra = divmod(total, count)
    start, out = 0, []
    for k in range(count):
        n = base + (1 if k < extra else 0)
        out.append((start, n))
        start += n
    return out


def gelu(x):
    inner = x * (0.7978845608028654 + 0.035677408136300125 * (x * x))
    half = 0.5 * x
    return half + half * jnp.tanh(inner)


def nt_dot(lhs, rhs):
    return lax.dot_general(lhs, rhs, (((1,), (1,)), ((), ())), preferred_element_type=F32)


def dot(lhs, rhs):
    return jnp.dot(lhs, rhs, preferred_element_type=F32)


def step_kernel(step, dims, *refs):
    members, nvars, cols, lat, hid = dims
    half = lat // 2
    coarse = cols // 2
    first, last = step == 0, step == STEPS - 1
    refs = list(refs)
    plan_ref, ids_ref, field_hbm, west, east = refs[:5]
    table_ref, wenc_hbm, wproc_hbm, wdec_hbm = refs[5:9]
    refs = refs[9 if first else 10 :]
    out_hbm = refs[0]
    refs = refs[1:]
    if not last:
        wedge_ref, eedge_ref = refs[:2]
        refs = refs[2:]
    (flds, wenc_ref, wproc, wdec_ref, halo) = refs[:5]
    (tmp, xe, xo, x1, x2, h0, h1, oo, sems, wsems) = refs[5:]

    def load_field(member):
        source = field_hbm.at[plan_ref[member]] if first else out_hbm.at[step - 1, member]
        return pltpu.make_async_copy(source, flds.at[member], sems.at[member])

    def save_field(member):
        return pltpu.make_async_copy(
            flds.at[member], out_hbm.at[step, member], sems.at[members + member]
        )

    load_enc = pltpu.make_async_copy(wenc_hbm, wenc_ref.at[:, 0 : 3 * VPAD], wsems.at[2])
    load_dec = pltpu.make_async_copy(wdec_hbm, wdec_ref, wsems.at[3])
    load_w = [
        [
            pltpu.make_async_copy(
                wproc_hbm.at[layer, a], wproc.at[layer, a], wsems.at[4 + 3 * layer + a]
            )
            for a in range(3)
        ]
        for layer in range(2)
    ]
    load_field(0).start()
    pick = (
        lax.broadcasted_iota(jnp.int32, (half, lat), 1)
        == 2 * lax.broadcasted_iota(jnp.int32, (half, lat), 0) + 1
    ).astype(F32).astype(BF16)
    lane = lax.broadcasted_iota(jnp.int32, (VPAD, lat), 1)
    tmp[...] = jnp.zeros(tmp.shape, F32)
    wenc_ref[:, 3 * VPAD :] = jnp.zeros((3, KENC - 3 * VPAD, hid), BF16)

    def take_in(index, values):
        buf = index % tmp.shape[0]
        tmp[buf, 0:nvars, :] = values
        values = tmp[buf]
        one = pltpu.roll(values, 1, 1)
        two = jnp.where(lane < 2, 0.0, pltpu.roll(values, 2, 1))
        stacked = jnp.concatenate(
            [two, one, values, jnp.zeros((KENC - 3 * VPAD, lat), F32)], axis=0
        ).astype(BF16)
        picked = nt_dot(pick, stacked).astype(BF16)
        target = xe if index % 2 == 0 else xo
        target[(index // 2) * half : (index // 2 + 1) * half, :] = picked

    def spread(values, ncols, start, dilation, target):
        rows = lax.broadcasted_iota(jnp.int32, (ncols * half, hid), 0) & (half - 1)
        down = jnp.where(rows < dilation, 0.0, pltpu.roll(values, dilation, 0))
        up = jnp.where(
            rows >= half - dilation, 0.0, pltpu.roll(values, ncols * half - dilation, 0)
        )
        where = slice(start * half, (start + ncols) * half)
        target[where, 0:hid] = down.astype(BF16)
        target[where, hid : 2 * hid] = values.astype(BF16)
        target[where, 2 * hid : 3 * hid] = up.astype(BF16)

    always = plan_ref[0] >= 0

    def alone(items):
        return [piece for _, piece in items]

    def evenly(items):
        return [((k + 0.5) / len(items), piece) for k, piece in enumerate(items)]

    def block(items):
        if not isinstance(items[0], tuple):
            items = evenly(items)

        @pl.when(always)
        def _():
            for _, piece in sorted(items, key=lambda item: item[0]):
                piece()

    def slot_of(member):
        return plan_ref[member] if first else member

    def open_halo(member):
        halo[0] = west[slot_of(member)].astype(F32)
        halo[1] = east[slot_of(member)].astype(F32)

    def intake(member):
        fld = flds.at[member]

        def own(p):
            take_in(WEST + p, fld[pl.ds(p, nvars, stride=cols), :])

        def from_west(p):
            take_in(p, halo[0, pl.ds(EDGE - WEST + p, nvars, stride=EDGE), :])

        def from_east(p):
            take_in(WEST + cols + p, halo[1, pl.ds(p, nvars, stride=EDGE), :])

        return (
            [functools.partial(from_west, p) for p in range(WEST)]
            + [functools.partial(own, p) for p in range(cols)]
            + [functools.partial(from_east, p) for p in range(EAST)]
        )

    def encode(member):
        def piece(start, n):
            mvec = table_ref[pl.ds(ids_ref[plan_ref[member]], 1), :]
            rows = slice(start * half, (start + n) * half)
            after = slice((start + 1) * half, (start + 1 + n) * half)
            hidden = dot(xe[rows, :], wenc_ref[0]) + dot(xo[rows, :], wenc_ref[1])
            hidden = hidden + dot(xe[after, :], wenc_ref[2]) + mvec
            lo, hi = max(start, 1), min(start + n, coarse + 6)
            h0[(lo - 1) * half : (hi - 1) * half, :] = hidden[
                (lo - start) * half : (hi - start) * half
            ]
            spread(gelu(hidden), n, start, 1, x1)

        return [(c, functools.partial(piece, *c)) for c in chunks(coarse + 7, 4)]

    def layer0():
        def piece(start, n):
            hidden = h0[start * half : (start + n) * half, :]
            for a in range(3):
                rows = slice((start + a) * half, (start + a + n) * half)
                hidden = hidden + dot(x1[rows, :], wproc[0, a])
            lo, hi = max(start, 2), min(start + n, coarse + 3)
            h1[(lo - 2) * half : (hi - 2) * half, :] = hidden[
                (lo - start) * half : (hi - start) * half
            ]
            spread(gelu(hidden), n, start, 2, x2)

        return [(c, functools.partial(piece, *c)) for c in chunks(coarse + 5, 4)]

    def layer1():
        def piece(start, n):
            hidden = h1[start * half : (start + n) * half, :]
            for a in range(3):
                rows = slice((start + 2 * a) * half, (start + 2 * a + n) * half)
                hidden = hidden + dot(x2[rows, :], wproc[1, a])
            outgoing = gelu(hidden)
            rows = lax.broadcasted_iota(jnp.int32, (n * half, hid), 0) & (half - 1)
            up = jnp.where(rows >= half - 1, 0.0, pltpu.roll(outgoing, n * half - 1, 0))
            where = slice(start * half, (start + n) * half)
            oo[where, 0:hid] = outgoing.astype(BF16)
            oo[where, hid : 2 * hid] = up.astype(BF16)

        return [(c, functools.partial(piece, *c)) for c in chunks(coarse + 1, 4)]

    def decode(member):
        fld = flds.at[member]

        def piece(start, n):
            key = lax.broadcasted_iota(jnp.int32, (2 * lat, 2 * lat), 0)
            spot = (key // half % 2) * lat + 2 * (key % half) + key // lat
            weave = lax.broadcasted_iota(jnp.int32, (2 * lat, 2 * lat), 1) == spot
            weave = weave.astype(F32).astype(BF16)
            v = VPAD
            here = slice(start * half, (start + n) * half)
            nxt = slice((start + 1) * half, (start + 1 + n) * half)
            tap = [wdec_ref[k * v : (k + 1) * v] for k in range(9)]
            g1 = nt_dot(jnp.concatenate([tap[4], tap[5], tap[7], tap[8]]), oo[here, 0:hid])
            g2 = nt_dot(jnp.concatenate([tap[3], tap[6]]), oo[here, hid : 2 * hid])
            g3 = nt_dot(jnp.concatenate([tap[1], tap[2]]), oo[nxt, 0:hid])
            g4 = nt_dot(tap[0], oo[nxt, hid : 2 * hid])
            parts = (
                (g1[0:v], g1[v : 2 * v] + g2[0:v]),
                (
                    g1[2 * v : 3 * v] + g3[0:v],
                    g1[3 * v : 4 * v] + g2[v : 2 * v] + g3[v : 2 * v] + g4,
                ),
            )
            for pair in range(n // 2):
                lanes = slice(pair * lat, (pair + 1) * lat)
                for lon_parity in range(2):
                    even, odd = parts[lon_parity]
                    both = jnp.concatenate([even[:, lanes], odd[:, lanes]], axis=1)
                    woven = dot(both.astype(BF16), weave)
                    for side in range(2):
                        p = 2 * (start + 2 * pair + side) + lon_parity
                        update = woven[:, side * lat : (side + 1) * lat]
                        there = pl.ds(p, nvars, stride=cols)
                        fld[there, :] = fld[there, :] + update[0:nvars]

        spans = [(2 * start, 2 * n) for start, n in chunks(coarse // 2, 2)]
        return [(c, functools.partial(piece, *c)) for c in spans]

    def close(member):
        save_field(member).start()
        if not last:
            fld = flds.at[member]
            for edge_ref, start in ((wedge_ref, 0), (eedge_ref, cols - EDGE)):
                rows = [fld[v * cols + start : v * cols + start + EDGE, :] for v in range(nvars)]
                edge_ref[member] = jnp.concatenate(rows, axis=0).astype(BF16)

    load_field(0).wait()
    load_enc.start()
    for load in load_w[0]:
        load.start()
    for member in range(1, members):
        load_field(member).start()
    open_halo(0)
    block(intake(0))
    load_enc.wait()
    block(alone(encode(0)))
    for load in load_w[0]:
        load.wait()
    for load in load_w[1]:
        load.start()
    load_dec.start()
    for member in range(members):
        beside = []
        if member + 1 < members:
            load_field(member + 1).wait()
            open_halo(member + 1)
            beside += evenly(intake(member + 1))
        if member > 0:
            beside += evenly(alone(decode(member - 1)))
        block(evenly(alone(layer0())) + beside)
        if member == 0:
            for load in load_w[1]:
                load.wait()
            load_dec.wait()
        else:
            close(member - 1)
        if member + 1 < members:
            beside = evenly(alone(encode(member + 1)))
            block(evenly(alone(layer1())) + beside)
        else:
            block(alone(layer1()))
            block(alone(decode(member)))
    close(members - 1)
    for member in range(members):
        save_field(member).wait()


def run_step(step, dims, plan, ids, field, west, east, table, wenc, wproc, wdec, buf):
    members, nvars, cols, lat, hid = dims
    half, coarse = lat // 2, cols // 2
    smem = pl.BlockSpec(memory_space=pltpu.SMEM)
    hbm = pl.BlockSpec(memory_space=pl.ANY)
    vmem = pl.BlockSpec(memory_space=pltpu.VMEM)
    args = [plan, ids, field, west, east, table, wenc, wproc, wdec]
    in_specs = [smem, smem, hbm, vmem, vmem, vmem, hbm, hbm, hbm]
    aliases = {}
    if buf is not None:
        aliases = {len(args): 0}
        args.append(buf)
        in_specs.append(hbm)
    out_shape = [jax.ShapeDtypeStruct((STEPS, members, nvars * cols, lat), F32)]
    out_specs = [hbm]
    if step < STEPS - 1:
        out_shape += [jax.ShapeDtypeStruct((members, nvars * EDGE, lat), BF16)] * 2
        out_specs += [vmem] * 2
    scratch = [
        pltpu.VMEM((members, nvars * cols, lat), F32),
        pltpu.VMEM((3, KENC, hid), BF16),
        pltpu.VMEM(wproc.shape, BF16),
        pltpu.VMEM(wdec.shape, BF16),
        pltpu.VMEM((2, nvars * EDGE, lat), F32),
        pltpu.VMEM((8, VPAD, lat), F32),
        pltpu.VMEM(((coarse + 8) * half, KENC), BF16),
        pltpu.VMEM(((coarse + 7) * half, KENC), BF16),
        pltpu.VMEM(((coarse + 7) * half, 3 * hid), BF16),
        pltpu.VMEM(((coarse + 5) * half, 3 * hid), BF16),
        pltpu.VMEM(((coarse + 5) * half, hid), F32),
        pltpu.VMEM(((coarse + 1) * half, hid), F32),
        pltpu.VMEM(((coarse + 1) * half, 2 * hid), BF16),
        pltpu.SemaphoreType.DMA((2 * members,)),
        pltpu.SemaphoreType.DMA((10,)),
    ]
    flops = members * 2 * half * hid * hid * 9 * (2 * coarse + 6)
    return pl.pallas_call(
        functools.partial(step_kernel, step, dims),
        out_shape=out_shape,
        in_specs=in_specs,
        out_specs=out_specs,
        scratch_shapes=scratch,
        input_output_aliases=aliases,
        cost_estimate=pl.CostEstimate(flops=flops, bytes_accessed=16 * 2**20, transcendentals=0),
        compiler_params=pltpu.CompilerParams(vmem_limit_bytes=44 * 2**20),
        name="rollout_step%d" % step,
    )(*args)


def exchange(last, first):
    count = lax.axis_size("space")
    forward = [(i, (i + 1) % count) for i in range(count)]
    backward = [(target, source) for source, target in forward]
    return lax.ppermute(last, "space", forward), lax.ppermute(first, "space", backward)


def local(states, plan, member_ids, member_table, enc_weight, proc_weight, dec_weight):
    members, nvars, cols, lat = states.shape
    hid = proc_weight.shape[-1]
    dims = (members, nvars, cols, lat, hid)

    pad_v = ((0, 0), (0, 0), (0, VPAD - nvars), (0, 0))
    wenc = jnp.pad(enc_weight, pad_v).reshape(3, 3 * VPAD, hid)
    wdec = jnp.pad(jnp.swapaxes(dec_weight, 2, 3), pad_v).reshape(9 * VPAD, hid)
    wproc = proc_weight.reshape(proc_weight.shape[0], 3, 3 * hid, hid)

    flat_edge = (members, nvars * EDGE, lat)
    west, east = exchange(
        states[:, :, cols - EDGE :].astype(BF16).reshape(flat_edge),
        states[:, :, :EDGE].astype(BF16).reshape(flat_edge),
    )
    flat = states.reshape(members, nvars * cols, lat)
    buf = None
    for step in range(STEPS):
        result = run_step(
            step, dims, plan, member_ids, flat, west, east, member_table, wenc, wproc, wdec, buf
        )
        buf = result[0]
        if step < STEPS - 1:
            west, east = exchange(result[2], result[1])
    return buf.reshape(STEPS, members, nvars, cols, lat)


def solution(mesh):
    return jax.shard_map(
        local,
        mesh=mesh,
        in_specs=(P("group", None, "space", None), P("group"), P("group"), P(), P(), P(), P()),
        out_specs=P(None, "group", None, "space", None),
        check_vma=False,
    )
```

```python
import functools

import jax
import jax.numpy as jnp
from jax import lax
from jax.experimental import pallas as pl
from jax.experimental.pallas import tpu as pltpu
from jax.sharding import PartitionSpec as P

STEPS = 2
VPAD = 80
WEST = 7
EAST = 8
EDGE = 8
KENC = 256
F32 = jnp.float32
BF16 = jnp.bfloat16


def chunks(total, size):
    count = max(1, total // size)
    base, extra = divmod(total, count)
    start, out = 0, []
    for k in range(count):
        n = base + (1 if k < extra else 0)
        out.append((start, n))
        start += n
    return out


def gelu(x):
    inner = x * (0.7978845608028654 + 0.035677408136300125 * (x * x))
    half = 0.5 * x
    return half + half * jnp.tanh(inner)


def nt_dot(lhs, rhs):
    return lax.dot_general(lhs, rhs, (((1,), (1,)), ((), ())), preferred_element_type=F32)


def dot(lhs, rhs):
    return jnp.dot(lhs, rhs, preferred_element_type=F32)


def step_kernel(step, dims, *refs):
    members, nvars, cols, lat, hid = dims
    half = lat // 2
    coarse = cols // 2
    first, last = step == 0, step == STEPS - 1
    refs = list(refs)
    plan_ref, ids_ref, field_hbm, west, east = refs[:5]
    table_ref, wenc_hbm, wproc_hbm, wdec_hbm = refs[5:9]
    refs = refs[9 if first else 10 :]
    out_hbm = refs[0]
    refs = refs[1:]
    if not last:
        wedge_ref, eedge_ref = refs[:2]
        refs = refs[2:]
    (flds, wenc_ref, wproc, wdec_ref, halo) = refs[:5]
    (tmp, xe, xo, x1, x2, h0, h1, oo, sems, wsems) = refs[5:]

    def load_field(member):
        source = field_hbm.at[plan_ref[member]] if first else out_hbm.at[step - 1, member]
        return pltpu.make_async_copy(source, flds.at[member], sems.at[member])

    def save_field(member):
        return pltpu.make_async_copy(
            flds.at[member], out_hbm.at[step, member], sems.at[members + member]
        )

    load_enc = pltpu.make_async_copy(wenc_hbm, wenc_ref.at[:, 0 : 3 * VPAD], wsems.at[2])
    load_dec = pltpu.make_async_copy(wdec_hbm, wdec_ref, wsems.at[3])
    load_w = [
        [
            pltpu.make_async_copy(
                wproc_hbm.at[layer, a], wproc.at[layer, a], wsems.at[4 + 3 * layer + a]
            )
            for a in range(3)
        ]
        for layer in range(2)
    ]
    load_field(0).start()
    pick = (
        lax.broadcasted_iota(jnp.int32, (half, lat), 1)
        == 2 * lax.broadcasted_iota(jnp.int32, (half, lat), 0) + 1
    ).astype(F32).astype(BF16)
    lane = lax.broadcasted_iota(jnp.int32, (VPAD, lat), 1)
    tmp[...] = jnp.zeros(tmp.shape, F32)
    wenc_ref[:, 3 * VPAD :] = jnp.zeros((3, KENC - 3 * VPAD, hid), BF16)

    def take_in(index, values):
        buf = index % tmp.shape[0]
        tmp[buf, 0:nvars, :] = values
        values = tmp[buf]
        one = pltpu.roll(values, 1, 1)
        two = jnp.where(lane < 2, 0.0, pltpu.roll(values, 2, 1))
        stacked = jnp.concatenate(
            [two, one, values, jnp.zeros((KENC - 3 * VPAD, lat), F32)], axis=0
        ).astype(BF16)
        picked = nt_dot(pick, stacked).astype(BF16)
        target = xe if index % 2 == 0 else xo
        target[(index // 2) * half : (index // 2 + 1) * half, :] = picked

    def spread(values, ncols, start, dilation, target):
        rows = lax.broadcasted_iota(jnp.int32, (ncols * half, hid), 0) & (half - 1)
        down = jnp.where(rows < dilation, 0.0, pltpu.roll(values, dilation, 0))
        up = jnp.where(
            rows >= half - dilation, 0.0, pltpu.roll(values, ncols * half - dilation, 0)
        )
        where = slice(start * half, (start + ncols) * half)
        target[where, 0:hid] = down.astype(BF16)
        target[where, hid : 2 * hid] = values.astype(BF16)
        target[where, 2 * hid : 3 * hid] = up.astype(BF16)

    always = plan_ref[0] >= 0

    def alone(items):
        return [piece for _, piece in items]

    def evenly(items):
        return [((k + 0.5) / len(items), piece) for k, piece in enumerate(items)]

    def block(items):
        if not isinstance(items[0], tuple):
            items = evenly(items)

        @pl.when(always)
        def _():
            for _, piece in sorted(items, key=lambda item: item[0]):
                piece()

    def slot_of(member):
        return plan_ref[member] if first else member

    def open_halo(member):
        halo[0] = west[slot_of(member)].astype(F32)
        halo[1] = east[slot_of(member)].astype(F32)

    def intake(member):
        fld = flds.at[member]

        def own(p):
            take_in(WEST + p, fld[pl.ds(p, nvars, stride=cols), :])

        def from_west(p):
            take_in(p, halo[0, pl.ds(EDGE - WEST + p, nvars, stride=EDGE), :])

        def from_east(p):
            take_in(WEST + cols + p, halo[1, pl.ds(p, nvars, stride=EDGE), :])

        return (
            [functools.partial(from_west, p) for p in range(WEST)]
            + [functools.partial(own, p) for p in range(cols)]
            + [functools.partial(from_east, p) for p in range(EAST)]
        )

    def encode(member):
        def piece(start, n):
            mvec = table_ref[pl.ds(ids_ref[plan_ref[member]], 1), :]
            rows = slice(start * half, (start + n) * half)
            after = slice((start + 1) * half, (start + 1 + n) * half)
            hidden = dot(xe[rows, :], wenc_ref[0]) + dot(xo[rows, :], wenc_ref[1])
            hidden = hidden + dot(xe[after, :], wenc_ref[2]) + mvec
            lo, hi = max(start, 1), min(start + n, coarse + 6)
            h0[(lo - 1) * half : (hi - 1) * half, :] = hidden[
                (lo - start) * half : (hi - start) * half
            ]
            spread(gelu(hidden), n, start, 1, x1)

        return [(c, functools.partial(piece, *c)) for c in chunks(coarse + 7, 4)]

    def layer0():
        def piece(start, n):
            hidden = h0[start * half : (start + n) * half, :]
            for a in range(3):
                rows = slice((start + a) * half, (start + a + n) * half)
                hidden = hidden + dot(x1[rows, :], wproc[0, a])
            lo, hi = max(start, 2), min(start + n, coarse + 3)
            h1[(lo - 2) * half : (hi - 2) * half, :] = hidden[
                (lo - start) * half : (hi - start) * half
            ]
            spread(gelu(hidden), n, start, 2, x2)

        return [(c, functools.partial(piece, *c)) for c in chunks(coarse + 5, 4)]

    def layer1():
        def piece(start, n):
            hidden = h1[start * half : (start + n) * half, :]
            for a in range(3):
                rows = slice((start + 2 * a) * half, (start + 2 * a + n) * half)
                hidden = hidden + dot(x2[rows, :], wproc[1, a])
            outgoing = gelu(hidden)
            rows = lax.broadcasted_iota(jnp.int32, (n * half, hid), 0) & (half - 1)
            up = jnp.where(rows >= half - 1, 0.0, pltpu.roll(outgoing, n * half - 1, 0))
            where = slice(start * half, (start + n) * half)
            oo[where, 0:hid] = outgoing.astype(BF16)
            oo[where, hid : 2 * hid] = up.astype(BF16)

        return [(c, functools.partial(piece, *c)) for c in chunks(coarse + 1, 4)]

    def decode(member):
        fld = flds.at[member]

        def piece(start, n):
            key = lax.broadcasted_iota(jnp.int32, (2 * lat, 2 * lat), 0)
            spot = (key // half % 2) * lat + 2 * (key % half) + key // lat
            weave = lax.broadcasted_iota(jnp.int32, (2 * lat, 2 * lat), 1) == spot
            weave = weave.astype(F32).astype(BF16)
            v = VPAD
            here = slice(start * half, (start + n) * half)
            nxt = slice((start + 1) * half, (start + 1 + n) * half)
            tap = [wdec_ref[k * v : (k + 1) * v] for k in range(9)]
            g1 = nt_dot(jnp.concatenate([tap[4], tap[5], tap[7], tap[8]]), oo[here, 0:hid])
            g2 = nt_dot(jnp.concatenate([tap[3], tap[6]]), oo[here, hid : 2 * hid])
            g3 = nt_dot(jnp.concatenate([tap[1], tap[2]]), oo[nxt, 0:hid])
            g4 = nt_dot(tap[0], oo[nxt, hid : 2 * hid])
            parts = (
                (g1[0:v], g1[v : 2 * v] + g2[0:v]),
                (
                    g1[2 * v : 3 * v] + g3[0:v],
                    g1[3 * v : 4 * v] + g2[v : 2 * v] + g3[v : 2 * v] + g4,
                ),
            )
            for pair in range(n // 2):
                lanes = slice(pair * lat, (pair + 1) * lat)
                for lon_parity in range(2):
                    even, odd = parts[lon_parity]
                    both = jnp.concatenate([even[:, lanes], odd[:, lanes]], axis=1)
                    woven = dot(both.astype(BF16), weave)
                    for side in range(2):
                        p = 2 * (start + 2 * pair + side) + lon_parity
                        update = woven[:, side * lat : (side + 1) * lat]
                        there = pl.ds(p, nvars, stride=cols)
                        fld[there, :] = fld[there, :] + update[0:nvars]

        spans = [(2 * start, 2 * n) for start, n in chunks(coarse // 2, 2)]
        return [(c, functools.partial(piece, *c)) for c in spans]

    def close(member):
        save_field(member).start()
        if not last:
            fld = flds.at[member]
            for edge_ref, start in ((wedge_ref, 0), (eedge_ref, cols - EDGE)):
                rows = [fld[v * cols + start : v * cols + start + EDGE, :] for v in range(nvars)]
                edge_ref[member] = jnp.concatenate(rows, axis=0).astype(BF16)

    def roll_out(member, carry):
        load_field(member).wait()

        @pl.when(member == 0)
        def weights():
            load_enc.start()
            for load in load_w[0]:
                load.start()
            for other in range(1, members):
                load_field(other).start()

        open_halo(member)
        block(intake(member))

        @pl.when(member == 0)
        def encoder_weight():
            load_enc.wait()

        block(alone(encode(member)))

        @pl.when(member == 0)
        def layer0_weight():
            for load in load_w[0]:
                load.wait()
            for load in load_w[1]:
                load.start()
            load_dec.start()

        block(alone(layer0()))

        @pl.when(member == 0)
        def layer1_weight():
            for load in load_w[1]:
                load.wait()
            load_dec.wait()

        block(alone(layer1()))
        block(alone(decode(member)))
        close(member)
        return carry

    lax.fori_loop(0, members, roll_out, 0)
    for member in range(members):
        save_field(member).wait()


def run_step(step, dims, plan, ids, field, west, east, table, wenc, wproc, wdec, buf):
    members, nvars, cols, lat, hid = dims
    half, coarse = lat // 2, cols // 2
    smem = pl.BlockSpec(memory_space=pltpu.SMEM)
    hbm = pl.BlockSpec(memory_space=pl.ANY)
    vmem = pl.BlockSpec(memory_space=pltpu.VMEM)
    args = [plan, ids, field, west, east, table, wenc, wproc, wdec]
    in_specs = [smem, smem, hbm, vmem, vmem, vmem, hbm, hbm, hbm]
    aliases = {}
    if buf is not None:
        aliases = {len(args): 0}
        args.append(buf)
        in_specs.append(hbm)
    out_shape = [jax.ShapeDtypeStruct((STEPS, members, nvars * cols, lat), F32)]
    out_specs = [hbm]
    if step < STEPS - 1:
        out_shape += [jax.ShapeDtypeStruct((members, nvars * EDGE, lat), BF16)] * 2
        out_specs += [vmem] * 2
    scratch = [
        pltpu.VMEM((members, nvars * cols, lat), F32),
        pltpu.VMEM((3, KENC, hid), BF16),
        pltpu.VMEM(wproc.shape, BF16),
        pltpu.VMEM(wdec.shape, BF16),
        pltpu.VMEM((2, nvars * EDGE, lat), F32),
        pltpu.VMEM((8, VPAD, lat), F32),
        pltpu.VMEM(((coarse + 8) * half, KENC), BF16),
        pltpu.VMEM(((coarse + 7) * half, KENC), BF16),
        pltpu.VMEM(((coarse + 7) * half, 3 * hid), BF16),
        pltpu.VMEM(((coarse + 5) * half, 3 * hid), BF16),
        pltpu.VMEM(((coarse + 5) * half, hid), F32),
        pltpu.VMEM(((coarse + 1) * half, hid), F32),
        pltpu.VMEM(((coarse + 1) * half, 2 * hid), BF16),
        pltpu.SemaphoreType.DMA((2 * members,)),
        pltpu.SemaphoreType.DMA((10,)),
    ]
    flops = members * 2 * half * hid * hid * 9 * (2 * coarse + 6)
    return pl.pallas_call(
        functools.partial(step_kernel, step, dims),
        out_shape=out_shape,
        in_specs=in_specs,
        out_specs=out_specs,
        scratch_shapes=scratch,
        input_output_aliases=aliases,
        cost_estimate=pl.CostEstimate(flops=flops, bytes_accessed=16 * 2**20, transcendentals=0),
        compiler_params=pltpu.CompilerParams(vmem_limit_bytes=44 * 2**20),
        name="rollout_step%d" % step,
    )(*args)


def exchange(last, first):
    count = lax.axis_size("space")
    forward = [(i, (i + 1) % count) for i in range(count)]
    backward = [(target, source) for source, target in forward]
    return lax.ppermute(last, "space", forward), lax.ppermute(first, "space", backward)


def local(states, plan, member_ids, member_table, enc_weight, proc_weight, dec_weight):
    members, nvars, cols, lat = states.shape
    hid = proc_weight.shape[-1]
    dims = (members, nvars, cols, lat, hid)

    pad_v = ((0, 0), (0, 0), (0, VPAD - nvars), (0, 0))
    wenc = jnp.pad(enc_weight, pad_v).reshape(3, 3 * VPAD, hid)
    wdec = jnp.pad(jnp.swapaxes(dec_weight, 2, 3), pad_v).reshape(9 * VPAD, hid)
    wproc = proc_weight.reshape(proc_weight.shape[0], 3, 3 * hid, hid)

    flat_edge = (members, nvars * EDGE, lat)
    west, east = exchange(
        states[:, :, cols - EDGE :].astype(BF16).reshape(flat_edge),
        states[:, :, :EDGE].astype(BF16).reshape(flat_edge),
    )
    flat = states.reshape(members, nvars * cols, lat)
    buf = None
    for step in range(STEPS):
        result = run_step(
            step, dims, plan, member_ids, flat, west, east, member_table, wenc, wproc, wdec, buf
        )
        buf = result[0]
        if step < STEPS - 1:
            west, east = exchange(result[2], result[1])
    return buf.reshape(STEPS, members, nvars, cols, lat)


def solution(mesh):
    return jax.shard_map(
        local,
        mesh=mesh,
        in_specs=(P("group", None, "space", None), P("group"), P("group"), P(), P(), P(), P()),
        out_specs=P(None, "group", None, "space", None),
        check_vma=False,
    )
```

```python
import functools

import jax
import jax.numpy as jnp
from jax import lax
from jax.experimental import pallas as pl
from jax.experimental.pallas import tpu as pltpu
from jax.sharding import PartitionSpec as P

STEPS = 2
VPAD = 80
WEST = 7
EAST = 8
EDGE = 8
KENC = 256
F32 = jnp.float32
BF16 = jnp.bfloat16


def chunks(total, size):
    count = max(1, total // size)
    base, extra = divmod(total, count)
    start, out = 0, []
    for k in range(count):
        n = base + (1 if k < extra else 0)
        out.append((start, n))
        start += n
    return out


def gelu(x):
    inner = x * (0.7978845608028654 + 0.035677408136300125 * (x * x))
    half = 0.5 * x
    return half + half * jnp.tanh(inner)


def nt_dot(lhs, rhs):
    return lax.dot_general(lhs, rhs, (((1,), (1,)), ((), ())), preferred_element_type=F32)


def dot(lhs, rhs):
    return jnp.dot(lhs, rhs, preferred_element_type=F32)


def step_kernel(step, dims, *refs):
    members, nvars, cols, lat, hid = dims
    half = lat // 2
    coarse = cols // 2
    first, last = step == 0, step == STEPS - 1
    refs = list(refs)
    plan_ref, ids_ref, field_hbm, west, east = refs[:5]
    table_ref, wenc_hbm, wproc_hbm, wdec_hbm = refs[5:9]
    refs = refs[9 if first else 10 :]
    out_hbm = refs[0]
    refs = refs[1:]
    if not last:
        wedge_ref, eedge_ref = refs[:2]
        refs = refs[2:]
    (flds, wenc_ref, wproc, wdec_ref, halo) = refs[:5]
    (tmp, xe, xo, x1, x2, h0, h1, oo, sems, wsems) = refs[5:]

    def load_field(member):
        source = field_hbm.at[plan_ref[member]] if first else out_hbm.at[step - 1, member]
        return pltpu.make_async_copy(source, flds.at[member], sems.at[member])

    def save_field(member):
        return pltpu.make_async_copy(
            flds.at[member], out_hbm.at[step, member], sems.at[members + member]
        )

    load_enc = pltpu.make_async_copy(wenc_hbm, wenc_ref.at[:, 0 : 3 * VPAD], wsems.at[2])
    load_dec = pltpu.make_async_copy(wdec_hbm, wdec_ref, wsems.at[3])
    load_w = [
        [
            pltpu.make_async_copy(
                wproc_hbm.at[layer, a], wproc.at[layer, a], wsems.at[4 + 3 * layer + a]
            )
            for a in range(3)
        ]
        for layer in range(2)
    ]
    load_field(0).start()
    pick = (
        lax.broadcasted_iota(jnp.int32, (half, lat), 1)
        == 2 * lax.broadcasted_iota(jnp.int32, (half, lat), 0) + 1
    ).astype(F32).astype(BF16)
    lane = lax.broadcasted_iota(jnp.int32, (VPAD, lat), 1)
    tmp[...] = jnp.zeros(tmp.shape, F32)
    wenc_ref[:, 3 * VPAD :] = jnp.zeros((3, KENC - 3 * VPAD, hid), BF16)

    def take_in(index, values):
        buf = index % tmp.shape[0]
        tmp[buf, 0:nvars, :] = values
        values = tmp[buf]
        one = pltpu.roll(values, 1, 1)
        two = jnp.where(lane < 2, 0.0, pltpu.roll(values, 2, 1))
        stacked = jnp.concatenate(
            [two, one, values, jnp.zeros((KENC - 3 * VPAD, lat), F32)], axis=0
        ).astype(BF16)
        picked = nt_dot(pick, stacked).astype(BF16)
        target = xe if index % 2 == 0 else xo
        target[(index // 2) * half : (index // 2 + 1) * half, :] = picked

    def spread(values, ncols, start, dilation, target):
        rows = lax.broadcasted_iota(jnp.int32, (ncols * half, hid), 0) & (half - 1)
        down = jnp.where(rows < dilation, 0.0, pltpu.roll(values, dilation, 0))
        up = jnp.where(
            rows >= half - dilation, 0.0, pltpu.roll(values, ncols * half - dilation, 0)
        )
        where = slice(start * half, (start + ncols) * half)
        target[where, 0:hid] = down.astype(BF16)
        target[where, hid : 2 * hid] = values.astype(BF16)
        target[where, 2 * hid : 3 * hid] = up.astype(BF16)

    always = plan_ref[0] >= 0

    def alone(items):
        return [piece for _, piece in items]

    def evenly(items):
        return [((k + 0.5) / len(items), piece) for k, piece in enumerate(items)]

    def block(items):
        if not isinstance(items[0], tuple):
            items = evenly(items)

        @pl.when(always)
        def _():
            for _, piece in sorted(items, key=lambda item: item[0]):
                piece()

    def slot_of(member):
        return plan_ref[member] if first else member

    def open_halo(member):
        halo[0] = west[slot_of(member)].astype(F32)
        halo[1] = east[slot_of(member)].astype(F32)

    def intake(member):
        fld = flds.at[member]

        def own(p):
            take_in(WEST + p, fld[pl.ds(p, nvars, stride=cols), :])

        def from_west(p):
            take_in(p, halo[0, pl.ds(EDGE - WEST + p, nvars, stride=EDGE), :])

        def from_east(p):
            take_in(WEST + cols + p, halo[1, pl.ds(p, nvars, stride=EDGE), :])

        return (
            [functools.partial(from_west, p) for p in range(WEST)]
            + [functools.partial(own, p) for p in range(cols)]
            + [functools.partial(from_east, p) for p in range(EAST)]
        )

    def encode(member):
        def piece(start, n):
            mvec = table_ref[pl.ds(ids_ref[plan_ref[member]], 1), :]
            rows = slice(start * half, (start + n) * half)
            after = slice((start + 1) * half, (start + 1 + n) * half)
            hidden = dot(xe[rows, :], wenc_ref[0]) + dot(xo[rows, :], wenc_ref[1])
            hidden = hidden + dot(xe[after, :], wenc_ref[2]) + mvec
            lo, hi = max(start, 1), min(start + n, coarse + 6)
            h0[(lo - 1) * half : (hi - 1) * half, :] = hidden[
                (lo - start) * half : (hi - start) * half
            ]
            spread(gelu(hidden), n, start, 1, x1)

        return [(c, functools.partial(piece, *c)) for c in chunks(coarse + 7, 3)]

    def layer0():
        def piece(start, n):
            hidden = h0[start * half : (start + n) * half, :]
            for a in range(3):
                rows = slice((start + a) * half, (start + a + n) * half)
                hidden = hidden + dot(x1[rows, :], wproc[0, a])
            lo, hi = max(start, 2), min(start + n, coarse + 3)
            h1[(lo - 2) * half : (hi - 2) * half, :] = hidden[
                (lo - start) * half : (hi - start) * half
            ]
            spread(gelu(hidden), n, start, 2, x2)

        return [(c, functools.partial(piece, *c)) for c in chunks(coarse + 5, 5)]

    def layer1():
        def piece(start, n):
            hidden = h1[start * half : (start + n) * half, :]
            for a in range(3):
                rows = slice((start + 2 * a) * half, (start + 2 * a + n) * half)
                hidden = hidden + dot(x2[rows, :], wproc[1, a])
            outgoing = gelu(hidden)
            rows = lax.broadcasted_iota(jnp.int32, (n * half, hid), 0) & (half - 1)
            up = jnp.where(rows >= half - 1, 0.0, pltpu.roll(outgoing, n * half - 1, 0))
            where = slice(start * half, (start + n) * half)
            oo[where, 0:hid] = outgoing.astype(BF16)
            oo[where, hid : 2 * hid] = up.astype(BF16)

        return [(c, functools.partial(piece, *c)) for c in chunks(coarse + 1, 4)]

    def decode(member):
        fld = flds.at[member]

        def piece(start, n):
            key = lax.broadcasted_iota(jnp.int32, (2 * lat, 2 * lat), 0)
            spot = (key // half % 2) * lat + 2 * (key % half) + key // lat
            weave = lax.broadcasted_iota(jnp.int32, (2 * lat, 2 * lat), 1) == spot
            weave = weave.astype(F32).astype(BF16)
            v = VPAD
            here = slice(start * half, (start + n) * half)
            nxt = slice((start + 1) * half, (start + 1 + n) * half)
            tap = [wdec_ref[k * v : (k + 1) * v] for k in range(9)]
            g1 = nt_dot(jnp.concatenate([tap[4], tap[5], tap[7], tap[8]]), oo[here, 0:hid])
            g2 = nt_dot(jnp.concatenate([tap[3], tap[6]]), oo[here, hid : 2 * hid])
            g3 = nt_dot(jnp.concatenate([tap[1], tap[2]]), oo[nxt, 0:hid])
            g4 = nt_dot(tap[0], oo[nxt, hid : 2 * hid])
            parts = (
                (g1[0:v], g1[v : 2 * v] + g2[0:v]),
                (
                    g1[2 * v : 3 * v] + g3[0:v],
                    g1[3 * v : 4 * v] + g2[v : 2 * v] + g3[v : 2 * v] + g4,
                ),
            )
            for pair in range(n // 2):
                lanes = slice(pair * lat, (pair + 1) * lat)
                for lon_parity in range(2):
                    even, odd = parts[lon_parity]
                    both = jnp.concatenate([even[:, lanes], odd[:, lanes]], axis=1)
                    woven = dot(both.astype(BF16), weave)
                    for side in range(2):
                        p = 2 * (start + 2 * pair + side) + lon_parity
                        update = woven[:, side * lat : (side + 1) * lat]
                        there = pl.ds(p, nvars, stride=cols)
                        fld[there, :] = fld[there, :] + update[0:nvars]

        spans = [(2 * start, 2 * n) for start, n in chunks(coarse // 2, 2)]
        return [(c, functools.partial(piece, *c)) for c in spans]

    def close(member):
        save_field(member).start()
        if not last:
            fld = flds.at[member]
            for edge_ref, start in ((wedge_ref, 0), (eedge_ref, cols - EDGE)):
                rows = [fld[v * cols + start : v * cols + start + EDGE, :] for v in range(nvars)]
                edge_ref[member] = jnp.concatenate(rows, axis=0).astype(BF16)

    def roll_out(member, carry):
        load_field(member).wait()

        @pl.when(member == 0)
        def weights():
            load_enc.start()
            for load in load_w[0]:
                load.start()
            for other in range(1, members):
                load_field(other).start()

        open_halo(member)
        block(intake(member))

        @pl.when(member == 0)
        def encoder_weight():
            load_enc.wait()

        block(alone(encode(member)))

        @pl.when(member == 0)
        def layer0_weight():
            for load in load_w[0]:
                load.wait()
            for load in load_w[1]:
                load.start()
            load_dec.start()

        block(alone(layer0()))

        @pl.when(member == 0)
        def layer1_weight():
            for load in load_w[1]:
                load.wait()
            load_dec.wait()

        block(alone(layer1()))
        block(alone(decode(member)))
        close(member)
        return carry

    lax.fori_loop(0, members, roll_out, 0)
    for member in range(members):
        save_field(member).wait()


def run_step(step, dims, plan, ids, field, west, east, table, wenc, wproc, wdec, buf):
    members, nvars, cols, lat, hid = dims
    half, coarse = lat // 2, cols // 2
    smem = pl.BlockSpec(memory_space=pltpu.SMEM)
    hbm = pl.BlockSpec(memory_space=pl.ANY)
    vmem = pl.BlockSpec(memory_space=pltpu.VMEM)
    args = [plan, ids, field, west, east, table, wenc, wproc, wdec]
    in_specs = [smem, smem, hbm, vmem, vmem, vmem, hbm, hbm, hbm]
    aliases = {}
    if buf is not None:
        aliases = {len(args): 0}
        args.append(buf)
        in_specs.append(hbm)
    out_shape = [jax.ShapeDtypeStruct((STEPS, members, nvars * cols, lat), F32)]
    out_specs = [hbm]
    if step < STEPS - 1:
        out_shape += [jax.ShapeDtypeStruct((members, nvars * EDGE, lat), BF16)] * 2
        out_specs += [vmem] * 2
    scratch = [
        pltpu.VMEM((members, nvars * cols, lat), F32),
        pltpu.VMEM((3, KENC, hid), BF16),
        pltpu.VMEM(wproc.shape, BF16),
        pltpu.VMEM(wdec.shape, BF16),
        pltpu.VMEM((2, nvars * EDGE, lat), F32),
        pltpu.VMEM((8, VPAD, lat), F32),
        pltpu.VMEM(((coarse + 8) * half, KENC), BF16),
        pltpu.VMEM(((coarse + 7) * half, KENC), BF16),
        pltpu.VMEM(((coarse + 7) * half, 3 * hid), BF16),
        pltpu.VMEM(((coarse + 5) * half, 3 * hid), BF16),
        pltpu.VMEM(((coarse + 5) * half, hid), F32),
        pltpu.VMEM(((coarse + 1) * half, hid), F32),
        pltpu.VMEM(((coarse + 1) * half, 2 * hid), BF16),
        pltpu.SemaphoreType.DMA((2 * members,)),
        pltpu.SemaphoreType.DMA((10,)),
    ]
    flops = members * 2 * half * hid * hid * 9 * (2 * coarse + 6)
    return pl.pallas_call(
        functools.partial(step_kernel, step, dims),
        out_shape=out_shape,
        in_specs=in_specs,
        out_specs=out_specs,
        scratch_shapes=scratch,
        input_output_aliases=aliases,
        cost_estimate=pl.CostEstimate(flops=flops, bytes_accessed=16 * 2**20, transcendentals=0),
        compiler_params=pltpu.CompilerParams(vmem_limit_bytes=44 * 2**20),
        name="rollout_step%d" % step,
    )(*args)


def exchange(last, first):
    count = lax.axis_size("space")
    forward = [(i, (i + 1) % count) for i in range(count)]
    backward = [(target, source) for source, target in forward]
    return lax.ppermute(last, "space", forward), lax.ppermute(first, "space", backward)


def local(states, plan, member_ids, member_table, enc_weight, proc_weight, dec_weight):
    members, nvars, cols, lat = states.shape
    hid = proc_weight.shape[-1]
    dims = (members, nvars, cols, lat, hid)

    pad_v = ((0, 0), (0, 0), (0, VPAD - nvars), (0, 0))
    wenc = jnp.pad(enc_weight, pad_v).reshape(3, 3 * VPAD, hid)
    wdec = jnp.pad(jnp.swapaxes(dec_weight, 2, 3), pad_v).reshape(9 * VPAD, hid)
    wproc = proc_weight.reshape(proc_weight.shape[0], 3, 3 * hid, hid)

    flat_edge = (members, nvars * EDGE, lat)
    ends = (states[:, :, cols - EDGE :], states[:, :, :EDGE])
    ends = lax.optimization_barrier(ends)
    west, east = exchange(*(end.astype(BF16).reshape(flat_edge) for end in ends))
    flat = states.reshape(members, nvars * cols, lat)
    buf = None
    for step in range(STEPS):
        result = run_step(
            step, dims, plan, member_ids, flat, west, east, member_table, wenc, wproc, wdec, buf
        )
        buf = result[0]
        if step < STEPS - 1:
            west, east = exchange(result[2], result[1])
    return buf.reshape(STEPS, members, nvars, cols, lat)


def solution(mesh):
    return jax.shard_map(
        local,
        mesh=mesh,
        in_specs=(P("group", None, "space", None), P("group"), P("group"), P(), P(), P(), P()),
        out_specs=P(None, "group", None, "space", None),
        check_vma=False,
    )
```
